32 devices in a mesh: groups: 1, dev: 32 (over z, y, x, core).
Axes of the slice: x: 2, y: 2, z: 4, core: 2. Of those that a mesh axis runs over, the one named last changes fastest.
Arguments:
- hidden_in: bfloat16 [128, 4096], P(('groups', 'dev')), may hold values from -6 to 6
- queries: bfloat16 [128, 8192], P(('groups', 'dev')), may hold values from -160 to 160
- kv_cache: bfloat16 [128, 256, 1024], P(('groups', 'dev')), may hold values from -6 to 6
- new_kv: bfloat16 [128, 1024], P(('groups', 'dev')), may hold values from -6 to 6
- seq_lengths: int32 [128], P(('groups', 'dev')), may hold values from 2 to 256
- o_weight: bfloat16 [8192, 4096], P('dev'), may hold values from -0.59765625 to 0.59765625
- norm_gain: float32 [4096], replicated, may hold values from 0.5 to 1.5
- route_ids: int32 [128, 8], P(('groups', 'dev')), may hold values from 0 to 15, all different within a row; in each aligned block of 4 rows (0 to 3, 4 to 7, ...) at most 2 rows name the same one
- route_weights: float32 [128, 8], P(('groups', 'dev')), may hold values from 0.05 to 0.5
- w_gate_up: bfloat16 [32, 4096, 768], P('dev'), may hold values from -0.09375 to 0.09375
- w_down: bfloat16 [32, 384, 4096], P('dev'), may hold values from -0.21875 to 0.21875
Outputs:
- layer_out: bfloat16 [128, 4096], P(('groups', 'dev'))
The draws below stay inside these ranges and needn't reach their ends.
Inputs may be any that keep to these rules, and one draw needn't show every extreme that they name: `route_ids`: a token names 8 different experts; in the rows of one device no expert is named by more than 2 tokens.
All inputs are finite; a program needn't handle non-finite values.
Results may differ from the reference program's by a relative error of at most 0.006.
Values may be sent and summed in bfloat16 or wider, within the bound.
A program may use at most 64 MiB of HBM per device.

```python
import math
import jax
import jax.numpy as jnp
import numpy as np
from jax import lax

D = 4096
HEADS = 64
KVH = 4
HD = 128
TOPK = 8
HSPLIT = 2
FF_DEV = 384
CTX = 256
SEQ_DEV = 4
FF = 768
E_WIN = 16
TOKENS = 128
MOST = 2
N_DEV = 32


def shared_cache(key):
    base = jax.random.normal(jax.random.fold_in(key, 101), (TOKENS, CTX, 2 * KVH * HD), jnp.float32)
    return jnp.clip(base, -6.0, 6.0)


def draw_kv_cache(key, part):
    base = shared_cache(key)
    return base.astype(jnp.bfloat16)


def draw_queries(key, part):
    key = jax.random.fold_in(key, 7)
    drawn = jnp.clip(jax.random.normal(key, (TOKENS, HEADS * HD), jnp.float32), -6.0, 6.0)
    return drawn.astype(jnp.bfloat16)


def draw_seq_lengths(key, part):
    key = jax.random.fold_in(key, 5)
    first_key, second_key = jax.random.split(key)
    lengths = jax.random.randint(first_key, (TOKENS,), 2, CTX + 1, dtype=jnp.int32)
    picked = jax.random.randint(second_key, (), 0, TOKENS, dtype=jnp.int32)
    return lengths.at[picked].set(CTX)


def block_levels(rng, extent, shards, smallest, top_value):
    loudness, own = 1.0, jax.random.fold_in(rng, 6)
    for axis_at, blocks in shards:
        steps = jnp.exp(jax.random.uniform(jax.random.fold_in(own, axis_at), (blocks,), jnp.float32, smallest / len(shards), top_value / len(shards)))
        loudness = loudness * jnp.repeat(steps, extent[axis_at] // blocks).reshape([-1 if axis == axis_at else 1 for axis in range(len(extent))])
    return loudness


def assign_block(rng, own, number, rows, amount, top, limit, slope):
    sequence = jax.random.permutation(rng, amount)
    heavy_load, common = portions_of(amount, rows * top, limit, slope, True), portions_of(amount, rows * top, limit, slope, False)
    places = jnp.arange(amount)

    def named(tallies, rotation):
        used = int((tallies > 0).sum())
        fixed = max(1, used // 4)
        shifted = fixed + (places - fixed + rotation * (used - fixed)) % max(1, amount - fixed)
        return jnp.zeros((amount,), jnp.int32).at[sequence[jnp.where(places < fixed, places, shifted)]].set(jnp.asarray(tallies, jnp.int32))

    tallies = jnp.where(number % 4 == 0, named(heavy_load, number // 4), named(common, number - number // 4 - 1))
    mixed = jax.random.permutation(jax.random.fold_in(own, 3), amount)
    donor, receiver = mixed[0:amount // 2 * 2:2], mixed[1:amount // 2 * 2:2]
    room = jnp.minimum(tallies[donor] - 1, limit - tallies[receiver]) // 2
    room = jnp.where((donor == sequence[0]) | (receiver == sequence[0]) | (tallies[receiver] == 0), 0, jnp.maximum(room, 0))
    shifted = jax.random.randint(jax.random.fold_in(own, 4), (amount // 2,), 0, 1 << 20) % (room + 1)
    tallies = tallies.at[donor].add(-shifted).at[receiver].add(shifted)
    items = jnp.searchsorted(jnp.cumsum(tallies), jnp.arange(rows * top), side="right").astype(jnp.int32)
    listing = items.reshape(top, rows).T
    listing = listing[jax.random.permutation(jax.random.fold_in(own, 1), rows)]
    rotation = jax.random.randint(jax.random.fold_in(own, 2), (rows, 1), 0, top)
    return jnp.take_along_axis(listing, (jnp.arange(top)[None, :] + rotation) % top, axis=1)


def portions_of(count, total, limit, skew, full):
    loads = [(1 << 20) // math.isqrt(rank ** skew) + 1 for rank in range(1, count + 1)]
    largest = limit if full else min(limit, max(-(-total // count), total * loads[0] // sum(loads)))
    least = 1 if total - largest >= count - 1 else 0
    counts, surplus = [largest] + [least] * (count - 1), total - largest - least * (count - 1)
    while surplus > 0:
        candidates = [i for i in range(1, count) if counts[i] < largest] or [i for i in range(1, count) if counts[i] < limit]
        whole, budget = sum([loads[i] for i in candidates]), surplus
        for i in candidates:
            extra = min(limit - counts[i], max(1, budget * loads[i] // whole), surplus)
            counts[i] = counts[i] + extra
            surplus = surplus - extra
    return np.array(counts)


def noise(rng, dims, deviation, reach, cuts=(), held_as=jnp.bfloat16):
    result = deviation * jax.random.normal(rng, dims, jnp.float32)
    if cuts:
        result = result * block_levels(rng, dims, cuts, -0.22, 0.18)
    return jnp.clip(result, -reach, reach).astype(held_as)


def setup_inputs(seed: int = 0, part: int = 0) -> dict:
    seeds = jax.random.split(jax.random.key(seed), 12)
    part_splits = jax.random.split(jax.random.fold_in(seeds[11], part), 12)
    hidden_in = noise(part_splits[0], (TOKENS, D), 1.0, 6.0, ((0, 32),))
    queries = draw_queries(jax.random.fold_in(jax.random.fold_in(seeds[11], part), 71), part)
    kv_cache = draw_kv_cache(jax.random.fold_in(jax.random.fold_in(seeds[11], part), 71), part)
    new_kv = noise(part_splits[3], (TOKENS, 2 * KVH * HD), 1.0, 6.0, ((0, 32),))
    seq_lengths = draw_seq_lengths(jax.random.fold_in(jax.random.fold_in(seeds[11], part), 71), part)
    o_weight = noise(seeds[5], (HEADS * HD, D), 0.1, 0.59765625, ((0, 32),))
    norm_gain = jnp.clip(1.0 + 0.1 * jax.random.normal(seeds[6], (D,), jnp.float32), 0.5, 1.5)
    route_ids_keys = jax.random.split(jax.random.fold_in(part_splits[7], 1), TOKENS // SEQ_DEV)
    route_ids_turns = jax.random.permutation(jax.random.fold_in(part_splits[7], 3), TOKENS // SEQ_DEV)
    route_ids = jax.vmap(lambda own, number: assign_block(jax.random.fold_in(part_splits[7], 2), own, number, SEQ_DEV, E_WIN, TOPK, MOST, 2))(route_ids_keys, route_ids_turns).reshape((TOKENS, TOPK))
    route_weights = jnp.clip(jnp.exp(math.log(0.5) - 2.3025851 * jax.random.uniform(part_splits[8], (TOKENS, TOPK), jnp.float32) ** block_levels(part_splits[8], (TOKENS, TOPK), ((0, 32),), -0.2, 0.2)), 0.05, 0.5)
    w_gate_up = noise(seeds[9], (N_DEV, D, 2 * FF_DEV), D ** -0.5, 0.09375, ((0, 32),))
    w_down = noise(seeds[10], (N_DEV, FF_DEV, D), FF ** -0.5, 0.21875, ((0, 32),))
    return {"hidden_in": hidden_in, "queries": queries, "kv_cache": kv_cache, "new_kv": new_kv, "seq_lengths": seq_lengths, "o_weight": o_weight, "norm_gain": norm_gain, "route_ids": route_ids, "route_weights": route_weights, "w_gate_up": w_gate_up, "w_down": w_down}


def attend(queries, kv_cache, new_kv, seq_lengths):
    seq_count = queries.shape[0]
    per_group = HEADS // KVH
    kv_width = KVH * HD
    score_scale = HD ** (-0.5)
    query_heads = queries.astype(jnp.float32).reshape(seq_count, KVH, per_group, HD)
    cache_keys = kv_cache[:, :, :kv_width].astype(jnp.float32).reshape(seq_count, CTX, KVH, HD)
    cache_values = kv_cache[:, :, kv_width:].astype(jnp.float32).reshape(seq_count, CTX, KVH, HD)
    fresh_key = new_kv[:, :kv_width].astype(jnp.float32).reshape(seq_count, KVH, HD)
    fresh_value = new_kv[:, kv_width:].astype(jnp.float32).reshape(seq_count, KVH, HD)
    cache_scores = jnp.einsum('bgqd,bjgd->bgqj', query_heads, cache_keys) * score_scale
    fresh_scores = jnp.einsum('bgqd,bgd->bgq', query_heads, fresh_key) * score_scale
    live_mask = jnp.arange(CTX, dtype=jnp.int32)[None, :] < seq_lengths[:, None]
    cache_scores = jnp.where(live_mask[:, None, None, :], cache_scores, -jnp.inf)
    peak_score = jnp.maximum(lax.optimization_barrier(jnp.max(cache_scores, axis=-1)), fresh_scores)
    cache_exp = jnp.exp(cache_scores - peak_score[..., None])
    fresh_exp = jnp.exp(fresh_scores - peak_score)
    denominator = lax.optimization_barrier(jnp.sum(cache_exp, axis=-1)) + fresh_exp
    cache_probs = (cache_exp / denominator[..., None]).astype(jnp.bfloat16)
    fresh_probs = (fresh_exp / denominator).astype(jnp.bfloat16)
    attended = jnp.einsum('bgqj,bjgd->bgqd', cache_probs.astype(jnp.float32), cache_values)
    attended = attended + fresh_probs.astype(jnp.float32)[..., None] * fresh_value[:, :, None, :]
    return attended.astype(jnp.bfloat16).reshape(seq_count, HEADS * HD)

def expert_half(normed, gate_up, down):
    gate_up_out = jnp.dot(normed, gate_up, preferred_element_type=jnp.float32)
    split_at = gate_up.shape[1] // 2
    activated = (jax.nn.silu(gate_up_out[:, :split_at]) * gate_up_out[:, split_at:]).astype(jnp.bfloat16)
    return jnp.dot(activated, down, preferred_element_type=jnp.float32).astype(jnp.bfloat16)

def reference(hidden_in, queries, kv_cache, new_kv, seq_lengths, o_weight, norm_gain, route_ids, route_weights, w_gate_up, w_down):
    attn = attend(queries, kv_cache, new_kv, seq_lengths)
    resid = hidden_in.astype(jnp.float32) + jnp.dot(attn, o_weight, preferred_element_type=jnp.float32)
    mean_square = lax.optimization_barrier(jnp.mean(resid * resid, axis=-1, keepdims=True))
    normed = (resid * lax.rsqrt(mean_square + 1e-06) * norm_gain).astype(jnp.bfloat16)

    def accumulate(running, slot_index):
        expert = slot_index // HSPLIT
        route_coef = lax.optimization_barrier(jnp.sum(jnp.where(route_ids == expert, route_weights, 0.0), axis=1))
        expert_out = expert_half(normed, w_gate_up[slot_index], w_down[slot_index])
        return (running + route_coef[:, None] * expert_out.astype(jnp.float32), None)
    routed_sum, _ = lax.scan(accumulate, jnp.zeros((TOKENS, D), jnp.float32), jnp.arange(N_DEV, dtype=jnp.int32))
    return (resid + routed_sum).astype(jnp.bfloat16)
```

```python
import functools

import jax
import jax.numpy as jnp
from jax import lax
from jax.experimental import pallas as pl
from jax.experimental.pallas import tpu as pltpu
from jax.sharding import PartitionSpec as P

HEADS = 64
KVH = 4
HD = 128
TOPK = 8
PLANE = 8
CHUNKS = 4
SUB = 4
F32 = jnp.float32
BF16 = jnp.bfloat16


def dev_copy(src, dst, send, recv, target):
    return pltpu.make_async_remote_copy(
        src_ref=src, dst_ref=dst, send_sem=send, recv_sem=recv,
        device_id={"dev": target}, device_id_type=pl.DeviceIdType.MESH,
    )


def pick_matrix(tokens, cols, block, offset, z_count):
    row = lax.broadcasted_iota(jnp.int32, (tokens, cols), 0)
    col = lax.broadcasted_iota(jnp.int32, (tokens, cols), 1)
    zr = z_count * 4
    b = row & 3
    z = (row >> 2) & (z_count - 1)
    rest = row // zr
    xy = rest & 3
    core = rest >> 2
    src = z * 8 + xy * 2 + core
    return jnp.where(col == src * block + offset + b, 1.0, 0.0).astype(BF16)


def kernel(
    n, lens, hid, q_ref, kv_hbm, new_ref, gain_ref, ids_ref, rw_ref, wo_hbm, wgu_hbm, wd_hbm,
    out_ref,
    kv, wo, wgu, wd, load_sem,
    asend, arecv, a_ss, a_rs, csend, crecv, c_ss, c_rs,
    yb, yf, crx, qf, qb, prx, zb, zf, zrx, res,
    core_ss, core_rs, pl_ss, pl_rs, z_ss, z_rs,
    nz, gx, nz_ss, nz_rs, np_ss, np_rs, nc_ss, nc_rs,
    gu, act, coef,
):
    me = lax.axis_index("dev")
    zc = n // PLANE
    zr = zc * 4
    tokens = 4 * n
    half = tokens // 2
    my_z = me // PLANE
    my_p = me % PLANE
    my_xy = my_p // 2
    my_core = my_p % 2
    mate = my_z * PLANE + my_xy * 2 + (1 - my_core)
    d_model = out_ref.shape[1]
    cw = d_model // CHUNKS
    sw = cw // SUB
    ctx = kv.shape[1]
    kvw = KVH * HD
    per_group = HEADS // KVH
    hpd = HEADS // n
    dpg = n // KVH
    block = asend.shape[1]

    def xy_peer(j):
        return my_z * PLANE + ((my_xy + j) % 4) * 2 + my_core

    def z_peer(j):
        return ((my_z + j) % zc) * PLANE + my_p

    barrier = pltpu.get_barrier_semaphore()

    loads = [
        pltpu.make_async_copy(kv_hbm, kv, load_sem.at[0]),
        pltpu.make_async_copy(wo_hbm, wo, load_sem.at[1]),
        pltpu.make_async_copy(wgu_hbm.at[0], wgu, load_sem.at[2]),
        pltpu.make_async_copy(wd_hbm.at[0], wd, load_sem.at[3]),
    ]
    loads[0].start()

    @pl.loop(1, n)
    def _(k):
        pl.semaphore_signal(
            barrier, inc=1, device_id={"dev": (me + k) % n}, device_id_type=pl.DeviceIdType.MESH
        )

    for load in loads[1:]:
        load.start()

    lane = lax.broadcasted_iota(jnp.int32, (4, 128), 1)
    ids = ids_ref[...]
    rw = rw_ref[...]
    own_coef = jnp.zeros((4, 128), F32)
    for k in range(TOPK):
        own_coef = own_coef + jnp.where(ids[:, k:k + 1] == (lane & 63), rw[:, k:k + 1], 0.0)
    high = own_coef.astype(BF16).astype(F32)
    packed = jnp.where(lane < 64, high, own_coef - high)
    csend[...] = jnp.concatenate([packed] * 4, axis=0).astype(BF16)

    rows = per_group * 4
    row_b = lax.broadcasted_iota(jnp.int32, (rows, 1), 0) & 3
    length = jnp.full((rows, 1), lens[0], jnp.int32)
    for b in range(1, 4):
        length = jnp.where(row_b == b, lens[b], length)
    live = lax.broadcasted_iota(jnp.int32, (rows, ctx), 1) < length
    new = new_ref[...].astype(F32)
    loads[0].wait()
    for g in range(KVH):
        q_all = q_ref[:, g * per_group * HD:(g + 1) * per_group * HD].astype(F32)
        qg = jnp.concatenate([q_all[:, r * HD:(r + 1) * HD] for r in range(per_group)], axis=0)
        k_own = jnp.concatenate([new[:, g * HD:(g + 1) * HD]] * per_group, axis=0)
        v_own = jnp.concatenate([new[:, kvw + g * HD:kvw + (g + 1) * HD]] * per_group, axis=0)
        q16 = qg.astype(BF16)
        scores = None
        for b in range(4):
            s_b = lax.dot_general(
                q16, kv[b, :, g * HD:(g + 1) * HD], (((1,), (1,)), ((), ())),
                preferred_element_type=F32,
            )
            scores = s_b if b == 0 else jnp.where(row_b == b, s_b, scores)
        scale = HD ** (-0.5)
        scores = jnp.where(live, scores * scale, -jnp.inf)
        fresh = jnp.sum(qg * k_own, axis=1, keepdims=True) * scale
        peak = jnp.maximum(jnp.max(scores, axis=1, keepdims=True), fresh)
        e = jnp.exp(scores - peak)
        e_own = jnp.exp(fresh - peak)
        den = jnp.sum(e, axis=1, keepdims=True) + e_own
        probs = e / den
        p_own = (e_own / den).astype(BF16).astype(F32)
        acc = p_own * v_own
        for b in range(4):
            p_b = jnp.where(row_b == b, probs, 0.0).astype(BF16)
            acc = acc + jnp.dot(
                p_b, kv[b, :, kvw + g * HD:kvw + (g + 1) * HD], preferred_element_type=F32
            )
        acc = acc.astype(BF16).astype(F32)
        for i in range(dpg):
            piece = acc[i * hpd * 4:(i + 1) * hpd * 4, :]
            if piece.shape[0] < block:
                piece = jnp.concatenate([piece] * (block // piece.shape[0]), axis=0)
            asend[g * dpg + i] = piece

        if g == 0:
            pl.semaphore_wait(barrier, n - 1)

            @pl.loop(1, n)
            def _(k):
                target = (me + k) % n
                dev_copy(csend, crecv.at[me], c_ss.at[target], c_rs.at[me], target).start()

        @pl.loop(0, dpg)
        def _(i):
            target = g * dpg + (me + i) % dpg

            @pl.when(target != me)
            def _():
                dev_copy(
                    asend.at[target], arecv.at[me], a_ss.at[target], a_rs.at[me], target
                ).start()

    arecv[me] = asend[me]
    crecv[me] = csend[...]

    @pl.loop(1, n)
    def _(k):
        source = (me + k) % n
        dev_copy(
            asend.at[source], arecv.at[source], a_ss.at[source], a_rs.at[source], source
        ).wait()

    x_all = arecv[...].reshape(n * block, HD).astype(BF16)
    gathered = jnp.concatenate(
        [
            jnp.dot(
                pick_matrix(tokens, n * block, block, rr * 4, zc), x_all,
                preferred_element_type=F32,
            )
            for rr in range(hpd)
        ],
        axis=1,
    ).astype(BF16)

    def reduce_chunks(t, make, done):
        cores = [
            dev_copy(yb.at[t, k, 1 - my_core], crx.at[t, k], core_ss.at[t, k], core_rs.at[t, k], mate)
            for k in range(CHUNKS)
        ]
        planes = [
            [
                dev_copy(
                    qb.at[t, k, (my_xy + j) % 4], prx.at[t, k, j - 1],
                    pl_ss.at[t, k, j - 1], pl_rs.at[t, k, j - 1], xy_peer(j),
                )
                for j in range(1, 4)
            ]
            for k in range(CHUNKS)
        ]
        lines = [
            [
                dev_copy(
                    zb.at[t, k, (my_z + j) % zc], zrx.at[t, k, j - 1],
                    z_ss.at[t, k, j - 1], z_rs.at[t, k, j - 1], z_peer(j),
                )
                for j in range(1, zc)
            ]
            for k in range(CHUNKS)
        ]
        for k in range(CHUNKS):
            y = make(k).reshape(2, 4, zr, cw)
            yb[t, k] = y.astype(BF16)
            cores[k].start()
            yf[k] = y
        for k in range(CHUNKS):
            cores[k].wait_recv()
            total = yf[k, my_core] + crx[t, k].astype(F32)
            qb[t, k] = total.astype(BF16)
            for copy in planes[k]:
                copy.start()
            qf[k] = total
        for k in range(CHUNKS):
            total = qf[k, my_xy]
            for j in range(1, 4):
                planes[k][j - 1].wait_recv()
                total = total + prx[t, k, j - 1].astype(F32)
            for z in range(zc):
                part = jnp.concatenate(
                    [total[4 * z:4 * z + 4, s * sw:(s + 1) * sw] for s in range(SUB)], axis=0
                )
                zb[t, k, z] = part.astype(BF16)
                zf[k, z] = part
            for copy in lines[k]:
                copy.start()
        for k in range(CHUNKS):
            total = zf[k, my_z]
            for j in range(1, zc):
                lines[k][j - 1].wait_recv()
                total = total + zrx[t, k, j - 1].astype(F32)
            done(k, total)
        for k in range(CHUNKS):
            cores[k].wait_send()
            for copy in planes[k] + lines[k]:
                copy.wait_send()

    loads[1].wait()

    def project(k):
        return jnp.dot(gathered, wo[:, k * cw:(k + 1) * cw], preferred_element_type=F32)

    hidden = hid[...].astype(F32)
    squares = []

    def add_hidden(k, total):
        own = jnp.concatenate(
            [hidden[:, k * cw + s * sw:k * cw + (s + 1) * sw] for s in range(SUB)], axis=0
        )
        value = total + own
        res[k] = value
        squares.append(jnp.sum(value * value, axis=1, keepdims=True))

    reduce_chunks(0, project, add_hidden)

    square = sum(squares[1:], squares[0])
    square = square[0:4] + square[4:8] + square[8:12] + square[12:16]
    inverse = lax.rsqrt(square / d_model + 1e-06)
    inverse = jnp.concatenate([inverse] * SUB, axis=0)

    line_out = []
    for k in range(CHUNKS):
        gain = jnp.concatenate(
            [
                jnp.broadcast_to(
                    gain_ref[:, k * cw + s * sw:k * cw + (s + 1) * sw], (4, sw)
                )
                for s in range(SUB)
            ],
            axis=0,
        )
        nz[k, my_z] = (res[k] * inverse * gain).astype(BF16)
        for j in range(1, zc):
            copy = dev_copy(
                nz.at[k, my_z], nz.at[k, my_z], nz_ss.at[k, j - 1], nz_rs.at[k, j - 1], z_peer(j)
            )
            copy.start()
            line_out.append(copy)
    plane_out = []
    for k in range(CHUNKS):
        for j in range(1, zc):
            from_z = (my_z + zc - j) % zc
            dev_copy(
                nz.at[k, from_z], nz.at[k, from_z], nz_ss.at[k, j - 1], nz_rs.at[k, j - 1], z_peer(j)
            ).wait_recv()
        parts = []
        for z in range(zc):
            value = nz[k, z].astype(F32)
            parts.append(
                jnp.concatenate([value[4 * s:4 * s + 4, :] for s in range(SUB)], axis=1)
            )
        gx[k, my_core, my_xy] = jnp.concatenate(parts, axis=0).astype(BF16)
        for j in range(1, 4):
            mine = gx.at[k, my_core, my_xy]
            copy = dev_copy(mine, mine, np_ss.at[k, j - 1], np_rs.at[k, j - 1], xy_peer(j))
            copy.start()
            plane_out.append(copy)
    core_out = []
    for k in range(CHUNKS):
        for j in range(1, 4):
            theirs = gx.at[k, my_core, (my_xy + 4 - j) % 4]
            dev_copy(theirs, theirs, np_ss.at[k, j - 1], np_rs.at[k, j - 1], xy_peer(j)).wait_recv()
        copy = dev_copy(gx.at[k, my_core], gx.at[k, my_core], nc_ss.at[k], nc_rs.at[k], mate)
        copy.start()
        core_out.append(copy)

    @pl.loop(1, n)
    def _(k):
        source = (me + k) % n
        dev_copy(csend, crecv.at[source], c_ss.at[source], c_rs.at[source], source).wait()

    spread = jnp.dot(
        pick_matrix(tokens, n * 16, 16, 0, zc), crecv[...].reshape(n * 16, 128),
        preferred_element_type=F32,
    )
    lane_t = lax.broadcasted_iota(jnp.int32, (tokens, 128), 1) & 63
    coef[...] = jnp.broadcast_to(
        jnp.sum(jnp.where(lane_t == me // 2, spread, 0.0), axis=1, keepdims=True), (tokens, 128)
    )

    loads[2].wait()
    for k in range(CHUNKS):
        mates = gx.at[k, 1 - my_core]
        dev_copy(mates, mates, nc_ss.at[k], nc_rs.at[k], mate).wait_recv()
        part = jnp.dot(
            gx[k].reshape(tokens, cw), wgu[k * cw:(k + 1) * cw, :], preferred_element_type=F32
        )
        if k == 0:
            gu[...] = part
        else:
            gu[...] += part
    for copy in line_out + plane_out + core_out:
        copy.wait_send()
    ff = gu.shape[1] // 2
    gate = gu[:, :ff]
    act[...] = (gate / (1.0 + jnp.exp(-gate)) * gu[:, ff:]).astype(BF16)

    loads[3].wait()

    def expert_out(k):
        y = jnp.dot(act[...], wd[:, k * cw:(k + 1) * cw], preferred_element_type=F32)
        return y.astype(BF16).astype(F32) * coef[:, 0:1]

    def finish(k, total):
        value = (res[k] + total).astype(out_ref.dtype).astype(F32)
        for s in range(SUB):
            lo = k * cw + s * sw
            out_ref[:, lo:lo + sw] = value[4 * s:4 * s + 4, :].astype(out_ref.dtype)

    reduce_chunks(1, expert_out, finish)


def solution(mesh):
    n = mesh.shape["dev"]

    def step(hidden, queries, kv_cache, new_kv, lens, wo, gain, ids, rw, wgu, wd):
        seqs, d_model = hidden.shape
        zc = n // PLANE
        zr = zc * 4
        tokens = n * seqs
        cw = d_model // CHUNKS
        sw = cw // SUB
        block = max(8, HEADS // n * 4)
        dma = pltpu.SemaphoreType.DMA
        vmem = pltpu.VMEM
        any_spec = pl.BlockSpec(memory_space=pl.ANY)
        v_spec = pl.BlockSpec(memory_space=pltpu.VMEM)
        zp = max(1, zc - 1)
        return pl.pallas_call(
            functools.partial(kernel, n),
            out_shape=jax.ShapeDtypeStruct((seqs, d_model), BF16),
            in_specs=[
                pl.BlockSpec(memory_space=pltpu.SMEM), v_spec, v_spec, any_spec, v_spec, v_spec,
                v_spec, v_spec, any_spec, any_spec, any_spec,
            ],
            out_specs=v_spec,
            scratch_shapes=[
                vmem(kv_cache.shape, BF16), vmem(wo.shape, BF16), vmem(wgu.shape[1:], BF16),
                vmem(wd.shape[1:], BF16), dma((4,)),
                vmem((n, block, HD), F32), vmem((n, block, HD), F32), dma((n,)), dma((n,)),
                vmem((16, 128), BF16), vmem((n, 16, 128), BF16), dma((n,)), dma((n,)),
                vmem((2, CHUNKS, 2, 4, zr, cw), BF16), vmem((CHUNKS, 2, 4, zr, cw), F32),
                vmem((2, CHUNKS, 4, zr, cw), BF16), vmem((CHUNKS, 4, zr, cw), F32),
                vmem((2, CHUNKS, 4, zr, cw), BF16), vmem((2, CHUNKS, 3, zr, cw), BF16),
                vmem((2, CHUNKS, zc, 4 * SUB, sw), BF16), vmem((CHUNKS, zc, 4 * SUB, sw), F32),
                vmem((2, CHUNKS, zp, 4 * SUB, sw), BF16), vmem((CHUNKS, 4 * SUB, sw), F32),
                dma((2, CHUNKS)), dma((2, CHUNKS)), dma((2, CHUNKS, 3)), dma((2, CHUNKS, 3)),
                dma((2, CHUNKS, zp)), dma((2, CHUNKS, zp)),
                vmem((CHUNKS, zc, 4 * SUB, sw), BF16), vmem((CHUNKS, 2, 4, zr, cw), BF16),
                dma((CHUNKS, zp)), dma((CHUNKS, zp)), dma((CHUNKS, 3)), dma((CHUNKS, 3)),
                dma((CHUNKS,)), dma((CHUNKS,)),
                vmem((tokens, wgu.shape[2]), F32), vmem((tokens, wgu.shape[2] // 2), BF16),
                vmem((tokens, 128), F32),
            ],
            compiler_params=pltpu.CompilerParams(
                collective_id=0, has_side_effects=True, vmem_limit_bytes=60 * 1024 * 1024
            ),
        )(lens, hidden, queries, kv_cache, new_kv, gain.reshape(1, d_model), ids, rw, wo, wgu, wd)

    tok = P(("groups", "dev"), None)
    in_specs = (
        tok, tok, P(("groups", "dev"), None, None), tok, P(("groups", "dev")), P("dev", None),
        P(), tok, tok, P("dev", None, None), P("dev", None, None),
    )
    return jax.shard_map(step, mesh=mesh, in_specs=in_specs, out_specs=tok, check_vma=False)
```

```python
import functools

import jax
import jax.numpy as jnp
from jax import lax
from jax.experimental import pallas as pl
from jax.experimental.pallas import tpu as pltpu
from jax.sharding import PartitionSpec as P

HEADS = 64
KVH = 4
HD = 128
TOPK = 8
PLANE = 8
CHUNKS = 4
SUB = 4
F32 = jnp.float32
BF16 = jnp.bfloat16


def dev_copy(src, dst, send, recv, target):
    return pltpu.make_async_remote_copy(
        src_ref=src, dst_ref=dst, send_sem=send, recv_sem=recv,
        device_id={"dev": target}, device_id_type=pl.DeviceIdType.MESH,
    )


def pick_matrix(tokens, cols, block, offset, z_count):
    row = lax.broadcasted_iota(jnp.int32, (tokens, cols), 0)
    col = lax.broadcasted_iota(jnp.int32, (tokens, cols), 1)
    zr = z_count * 4
    b = row & 3
    z = (row >> 2) & (z_count - 1)
    rest = row // zr
    second = rest & 1
    first = (rest >> 1) & 1
    core = rest >> 2
    x = jnp.where(core == 0, first, second)
    y = jnp.where(core == 0, second, first)
    src = z * 8 + y * 4 + x * 2 + core
    return jnp.where(col == src * block + offset + b, 1.0, 0.0).astype(BF16)


def kernel(
    n, lens, hid_hbm, q_hbm, kv_hbm, new_hbm, gain_hbm, ids_hbm, rw_hbm, wo_hbm, wgu_hbm, wd_hbm,
    out_ref,
    hid, q_ref, new_ref, gain_ref, ids_ref, rw_ref, kv, wo, wgu, wd, load_sem,
    asend, arecv, a_ss, a_rs,
    cz, cg, cz_ss, cz_rs, cg_ss, cg_rs,
    yb, yf, crx, qf, qb, p1rx, q2f, q2b, p2rx, zb, zf, zrx, res,
    rs_ss, rs_rs, z_ss, z_rs,
    nz, gx, nz_ss, nz_rs, ag_ss, ag_rs,
    gu, act, coef,
):
    me = lax.axis_index("dev")
    zc = n // PLANE
    zr = zc * 4
    tokens = 4 * n
    half = tokens // 2
    my_z = lax.div(me, PLANE)
    my_p = lax.rem(me, PLANE)
    my_y = lax.div(my_p, 4)
    my_x = lax.rem(lax.div(my_p, 2), 2)
    my_core = lax.rem(my_p, 2)
    first = (1 - my_core) * my_x + my_core * my_y
    second = (1 - my_core) * my_y + my_core * my_x
    step_x = (1 - 2 * my_x) * 2
    step_y = (1 - 2 * my_y) * 4
    peer1 = me + (1 - my_core) * step_x + my_core * step_y
    peer2 = me + (1 - my_core) * step_y + my_core * step_x
    mate = me + 1 - 2 * my_core
    d_model = out_ref.shape[1]
    cw = d_model // CHUNKS
    sw = cw // SUB
    ctx = kv.shape[1]
    kvw = KVH * HD
    per_group = HEADS // KVH
    hpd = HEADS // n
    dpg = n // KVH
    block = asend.shape[1]

    def z_at(j):
        return lax.rem(my_z + j, zc)

    def z_peer(j):
        return z_at(j) * PLANE + my_p

    barrier = pltpu.get_barrier_semaphore()

    @pl.loop(1, n)
    def _(k):
        pl.semaphore_signal(
            barrier, inc=1, device_id={"dev": lax.rem(me + k, n)},
            device_id_type=pl.DeviceIdType.MESH,
        )

    small = [
        pltpu.make_async_copy(src, dst, load_sem.at[i])
        for i, (src, dst) in enumerate(
            [
                (q_hbm, q_ref), (new_hbm, new_ref), (ids_hbm, ids_ref), (rw_hbm, rw_ref),
                (kv_hbm, kv), (hid_hbm, hid), (gain_hbm, gain_ref),
            ]
        )
    ]
    loads = [
        pltpu.make_async_copy(wo_hbm, wo, load_sem.at[7]),
        pltpu.make_async_copy(wgu_hbm.at[0], wgu, load_sem.at[8]),
        pltpu.make_async_copy(wd_hbm.at[0], wd, load_sem.at[9]),
    ]
    for load in small + loads:
        load.start()
    for load in small[:4]:
        load.wait()

    lane = lax.broadcasted_iota(jnp.int32, (4, 128), 1)
    ids = ids_ref[...]
    rw = rw_ref[...]
    own_coef = jnp.zeros((4, 128), F32)
    for k in range(TOPK):
        own_coef = own_coef + jnp.where(ids[:, k:k + 1] == (lane & 63), rw[:, k:k + 1], 0.0)
    high = own_coef.astype(BF16).astype(F32)
    packed = jnp.where(lane < 64, high, own_coef - high)
    cz[my_z] = jnp.concatenate([packed] * 4, axis=0).astype(BF16)

    rows = per_group * 4
    row_b = lax.broadcasted_iota(jnp.int32, (rows, 1), 0) & 3
    length = jnp.full((rows, 1), lens[0], jnp.int32)
    for b in range(1, 4):
        length = jnp.where(row_b == b, lens[b], length)
    live = lax.broadcasted_iota(jnp.int32, (rows, ctx), 1) < length
    new = new_ref[...].astype(F32)
    for load in small[4:]:
        load.wait()
    for g in range(KVH):
        q_all = q_ref[:, g * per_group * HD:(g + 1) * per_group * HD].astype(F32)
        qg = jnp.concatenate([q_all[:, r * HD:(r + 1) * HD] for r in range(per_group)], axis=0)
        k_own = jnp.concatenate([new[:, g * HD:(g + 1) * HD]] * per_group, axis=0)
        v_own = jnp.concatenate([new[:, kvw + g * HD:kvw + (g + 1) * HD]] * per_group, axis=0)
        q16 = qg.astype(BF16)
        scores = None
        for b in range(4):
            s_b = lax.dot_general(
                q16, kv[b, :, g * HD:(g + 1) * HD], (((1,), (1,)), ((), ())),
                preferred_element_type=F32,
            )
            scores = s_b if b == 0 else jnp.where(row_b == b, s_b, scores)
        scale = HD ** (-0.5)
        scores = jnp.where(live, scores * scale, -jnp.inf)
        fresh = jnp.sum(qg * k_own, axis=1, keepdims=True) * scale
        peak = jnp.maximum(jnp.max(scores, axis=1, keepdims=True), fresh)
        e = jnp.exp(scores - peak)
        e_own = jnp.exp(fresh - peak)
        den = jnp.sum(e, axis=1, keepdims=True) + e_own
        probs = e / den
        p_own = (e_own / den).astype(BF16).astype(F32)
        acc = p_own * v_own
        for b in range(4):
            p_b = jnp.where(row_b == b, probs, 0.0).astype(BF16)
            acc = acc + jnp.dot(
                p_b, kv[b, :, kvw + g * HD:kvw + (g + 1) * HD], preferred_element_type=F32
            )
        for i in range(dpg):
            piece = acc[i * hpd * 4:(i + 1) * hpd * 4, :]
            if piece.shape[0] < block:
                piece = jnp.concatenate([piece] * (block // piece.shape[0]), axis=0)
            asend[g * dpg + i] = piece.astype(BF16)

    pl.semaphore_wait(barrier, n - 1)

    @pl.loop(1, n)
    def _(k):
        target = lax.rem(me + k, n)
        dev_copy(asend.at[target], arecv.at[me], a_ss.at[target], a_rs.at[me], target).start()

    coef_out = []
    for j in range(1, zc):
        copy = dev_copy(
            cz.at[my_z], cz.at[my_z], cz_ss.at[j - 1], cz_rs.at[j - 1], z_peer(j)
        )
        copy.start()
        coef_out.append(copy)

    arecv[me] = asend[me]

    @pl.loop(1, n)
    def _(k):
        source = lax.rem(me + k, n)
        dev_copy(
            asend.at[source], arecv.at[source], a_ss.at[source], a_rs.at[source], source
        ).wait()

    x_all = arecv[...].astype(F32).reshape(n * block, HD).astype(BF16)
    gathered = jnp.concatenate(
        [
            jnp.dot(
                pick_matrix(tokens, n * block, block, rr * 4, zc), x_all,
                preferred_element_type=F32,
            )
            for rr in range(hpd)
        ],
        axis=1,
    ).astype(BF16)

    def reduce_chunks(t, make, done):
        ks = range(CHUNKS)
        cores = [
            dev_copy(
                yb.at[t, k, 1 - my_core], crx.at[t, k], rs_ss.at[t, k, 0], rs_rs.at[t, k, 0], mate
            )
            for k in ks
        ]
        firsts = [
            dev_copy(
                qb.at[t, k, 1 - first], p1rx.at[t, k], rs_ss.at[t, k, 1], rs_rs.at[t, k, 1], peer1
            )
            for k in ks
        ]
        seconds = [
            dev_copy(
                q2b.at[t, k, 1 - second], p2rx.at[t, k], rs_ss.at[t, k, 2], rs_rs.at[t, k, 2], peer2
            )
            for k in ks
        ]
        lines = [
            [
                dev_copy(
                    zb.at[t, k, z_at(j)], zrx.at[t, k, j - 1],
                    z_ss.at[t, k, j - 1], z_rs.at[t, k, j - 1], z_peer(j),
                )
                for j in range(1, zc)
            ]
            for k in range(CHUNKS)
        ]
        for k in range(CHUNKS):
            y = make(k).reshape(2, 2, 2, zr, cw)
            yb[t, k] = y.astype(BF16)
            cores[k].start()
            yf[k] = y
        for k in range(CHUNKS):
            cores[k].wait_recv()
            total = yf[k, my_core] + crx[t, k].astype(F32)
            qb[t, k] = total.astype(BF16)
            firsts[k].start()
            qf[k] = total
        for k in range(CHUNKS):
            firsts[k].wait_recv()
            total = qf[k, first] + p1rx[t, k].astype(F32)
            q2b[t, k] = total.astype(BF16)
            seconds[k].start()
            q2f[k] = total
        for k in range(CHUNKS):
            seconds[k].wait_recv()
            total = q2f[k, second] + p2rx[t, k].astype(F32)
            for z in range(zc):
                part = jnp.concatenate(
                    [total[4 * z:4 * z + 4, s * sw:(s + 1) * sw] for s in range(SUB)], axis=0
                )
                zb[t, k, z] = part.astype(BF16)
                zf[k, z] = part
            for copy in lines[k]:
                copy.start()
        for k in range(CHUNKS):
            total = zf[k, my_z]
            for j in range(1, zc):
                lines[k][j - 1].wait_recv()
                total = total + zrx[t, k, j - 1].astype(F32)
            done(k, total)
        for k in range(CHUNKS):
            for copy in [cores[k], firsts[k], seconds[k]] + lines[k]:
                copy.wait_send()

    for j in range(1, zc):
        from_z = z_at(zc - j)
        dev_copy(
            cz.at[from_z], cz.at[from_z], cz_ss.at[j - 1], cz_rs.at[j - 1], z_peer(j)
        ).wait_recv()
    cg[my_core, first, second] = jnp.concatenate(
        [cz[z].astype(F32)[0:4, :] for z in range(zc)], axis=0
    ).astype(BF16)

    def spread(ref, stage, send, recv):
        here, there, target = [
            (ref.at[my_core, first, second], ref.at[my_core, first, 1 - second], peer2),
            (ref.at[my_core, first], ref.at[my_core, 1 - first], peer1),
            (ref.at[my_core], ref.at[1 - my_core], mate),
        ][stage]
        out = dev_copy(here, here, send, recv, target)
        arrive = dev_copy(there, there, send, recv, target)
        return out, arrive

    coef_steps = [spread(cg, i, cg_ss.at[i], cg_rs.at[i]) for i in range(3)]
    coef_steps[0][0].start()

    loads[0].wait()

    def project(k):
        return jnp.dot(gathered, wo[:, k * cw:(k + 1) * cw], preferred_element_type=F32)

    hidden = hid[...].astype(F32)
    squares = []

    def add_hidden(k, total):
        own = jnp.concatenate(
            [hidden[:, k * cw + s * sw:k * cw + (s + 1) * sw] for s in range(SUB)], axis=0
        )
        value = total + own
        res[k] = value
        squares.append(jnp.sum(value * value, axis=1, keepdims=True))

    reduce_chunks(0, project, add_hidden)

    coef_steps[0][1].wait_recv()
    coef_steps[1][0].start()
    square = sum(squares[1:], squares[0])
    square = square[0:4] + square[4:8] + square[8:12] + square[12:16]
    inverse = lax.rsqrt(square / d_model + 1e-06)
    inverse = jnp.concatenate([inverse] * SUB, axis=0)

    line_out = []
    for k in range(CHUNKS):
        gain = jnp.concatenate(
            [
                jnp.broadcast_to(
                    gain_ref[:, k * cw + s * sw:k * cw + (s + 1) * sw], (4, sw)
                )
                for s in range(SUB)
            ],
            axis=0,
        )
        nz[k, my_z] = (res[k] * inverse * gain).astype(BF16)
        for j in range(1, zc):
            copy = dev_copy(
                nz.at[k, my_z], nz.at[k, my_z], nz_ss.at[k, j - 1], nz_rs.at[k, j - 1], z_peer(j)
            )
            copy.start()
            line_out.append(copy)
    steps = [
        [spread(gx.at[k], i, ag_ss.at[k, i], ag_rs.at[k, i]) for i in range(3)]
        for k in range(CHUNKS)
    ]
    for k in range(CHUNKS):
        for j in range(1, zc):
            from_z = z_at(zc - j)
            dev_copy(
                nz.at[k, from_z], nz.at[k, from_z], nz_ss.at[k, j - 1], nz_rs.at[k, j - 1], z_peer(j)
            ).wait_recv()
        parts = []
        for z in range(zc):
            value = nz[k, z].astype(F32)
            parts.append(
                jnp.concatenate([value[4 * s:4 * s + 4, :] for s in range(SUB)], axis=1)
            )
        gx[k, my_core, first, second] = jnp.concatenate(parts, axis=0).astype(BF16)
        steps[k][0][0].start()
    coef_steps[1][1].wait_recv()
    coef_steps[2][0].start()
    for stage in (1, 2):
        for k in range(CHUNKS):
            steps[k][stage - 1][1].wait_recv()
            steps[k][stage][0].start()

    coef_steps[2][1].wait_recv()
    lane_t = lax.broadcasted_iota(jnp.int32, (tokens, 128), 1) & 63
    all_coef = cg[...].reshape(tokens, 128).astype(F32)
    coef[...] = jnp.broadcast_to(
        jnp.sum(
            jnp.where(lane_t == lax.div(me, 2), all_coef, 0.0), axis=1, keepdims=True
        ),
        (tokens, 128),
    )

    loads[1].wait()
    for k in range(CHUNKS):
        steps[k][2][1].wait_recv()
        part = jnp.dot(
            gx[k].reshape(tokens, cw), wgu[k * cw:(k + 1) * cw, :], preferred_element_type=F32
        )
        if k == 0:
            gu[...] = part
        else:
            gu[...] += part
    for copy in line_out + coef_out:
        copy.wait_send()
    for group in steps + [coef_steps]:
        for out, _ in group:
            out.wait_send()
    ff = gu.shape[1] // 2
    gate = gu[:, :ff]
    act[...] = (gate / (1.0 + jnp.exp(-gate)) * gu[:, ff:]).astype(BF16)

    loads[2].wait()

    def expert_out(k):
        y = jnp.dot(act[...], wd[:, k * cw:(k + 1) * cw], preferred_element_type=F32)
        return y.astype(BF16).astype(F32) * coef[:, 0:1]

    def finish(k, total):
        value = (res[k] + total).astype(out_ref.dtype).astype(F32)
        for s in range(SUB):
            lo = k * cw + s * sw
            out_ref[:, lo:lo + sw] = value[4 * s:4 * s + 4, :].astype(out_ref.dtype)

    reduce_chunks(1, expert_out, finish)


def solution(mesh):
    n = mesh.shape["dev"]

    def step(hidden, queries, kv_cache, new_kv, lens, wo, gain, ids, rw, wgu, wd):
        seqs, d_model = hidden.shape
        zc = n // PLANE
        zr = zc * 4
        tokens = n * seqs
        cw = d_model // CHUNKS
        sw = cw // SUB
        block = max(8, HEADS // n * 4)
        dma = pltpu.SemaphoreType.DMA
        vmem = pltpu.VMEM
        any_spec = pl.BlockSpec(memory_space=pl.ANY)
        v_spec = pl.BlockSpec(memory_space=pltpu.VMEM)
        zp = max(1, zc - 1)
        return pl.pallas_call(
            functools.partial(kernel, n),
            out_shape=jax.ShapeDtypeStruct((seqs, d_model), BF16),
            in_specs=[pl.BlockSpec(memory_space=pltpu.SMEM)] + [any_spec] * 10,
            out_specs=v_spec,
            scratch_shapes=[
                vmem(hidden.shape, BF16), vmem(queries.shape, BF16), vmem(new_kv.shape, BF16),
                vmem((1, d_model), F32), vmem(ids.shape, jnp.int32), vmem(rw.shape, F32),
                vmem(kv_cache.shape, BF16), vmem(wo.shape, BF16), vmem(wgu.shape[1:], BF16),
                vmem(wd.shape[1:], BF16), dma((10,)),
                vmem((n, block, HD), BF16), vmem((n, block, HD), BF16), dma((n,)), dma((n,)),
                vmem((zc, 16, 128), BF16), vmem((2, 2, 2, zr, 128), BF16),
                dma((zp,)), dma((zp,)), dma((3,)), dma((3,)),
                vmem((2, CHUNKS, 2, 2, 2, zr, cw), BF16), vmem((CHUNKS, 2, 2, 2, zr, cw), F32),
                vmem((2, CHUNKS, 2, 2, zr, cw), BF16), vmem((CHUNKS, 2, 2, zr, cw), F32),
                vmem((2, CHUNKS, 2, 2, zr, cw), BF16), vmem((2, CHUNKS, 2, zr, cw), BF16),
                vmem((CHUNKS, 2, zr, cw), F32), vmem((2, CHUNKS, 2, zr, cw), BF16),
                vmem((2, CHUNKS, zr, cw), BF16),
                vmem((2, CHUNKS, zc, 4 * SUB, sw), BF16), vmem((CHUNKS, zc, 4 * SUB, sw), F32),
                vmem((2, CHUNKS, zp, 4 * SUB, sw), BF16), vmem((CHUNKS, 4 * SUB, sw), F32),
                dma((2, CHUNKS, 3)), dma((2, CHUNKS, 3)), dma((2, CHUNKS, zp)), dma((2, CHUNKS, zp)),
                vmem((CHUNKS, zc, 4 * SUB, sw), BF16), vmem((CHUNKS, 2, 2, 2, zr, cw), BF16),
                dma((CHUNKS, zp)), dma((CHUNKS, zp)), dma((CHUNKS, 3)), dma((CHUNKS, 3)),
                vmem((tokens, wgu.shape[2]), F32), vmem((tokens, wgu.shape[2] // 2), BF16),
                vmem((tokens, 128), F32),
            ],
            compiler_params=pltpu.CompilerParams(
                collective_id=0, has_side_effects=True, vmem_limit_bytes=60 * 1024 * 1024
            ),
        )(lens, hidden, queries, kv_cache, new_kv, gain.reshape(1, d_model), ids, rw, wo, wgu, wd)

    tok = P(("groups", "dev"), None)
    in_specs = (
        tok, tok, P(("groups", "dev"), None, None), tok, P(("groups", "dev")), P("dev", None),
        P(), tok, tok, P("dev", None, None), P("dev", None, None),
    )
    return jax.shard_map(step, mesh=mesh, in_specs=in_specs, out_specs=tok, check_vma=False)
```

```python
import functools

import jax
import jax.numpy as jnp
from jax import lax
from jax.experimental import pallas as pl
from jax.experimental.pallas import tpu as pltpu
from jax.sharding import PartitionSpec as P

HEADS = 64
KVH = 4
HD = 128
TOPK = 8
PLANE = 8
CHUNKS = 4
SUB = 4
F32 = jnp.float32
BF16 = jnp.bfloat16


def dev_copy(src, dst, send, recv, target):
    return pltpu.make_async_remote_copy(
        src_ref=src, dst_ref=dst, send_sem=send, recv_sem=recv,
        device_id={"dev": target}, device_id_type=pl.DeviceIdType.MESH,
    )


def pick_matrix(tokens, cols, block, offset, z_count):
    row = lax.broadcasted_iota(jnp.int32, (tokens, cols), 0)
    col = lax.broadcasted_iota(jnp.int32, (tokens, cols), 1)
    zr = z_count * 4
    b = row & 3
    z = (row >> 2) & (z_count - 1)
    rest = row // zr
    second = rest & 1
    first = (rest >> 1) & 1
    core = rest >> 2
    x = jnp.where(core == 0, first, second)
    y = jnp.where(core == 0, second, first)
    src = z * 8 + y * 4 + x * 2 + core
    return jnp.where(col == src * block + offset + b, 1.0, 0.0).astype(BF16)


def kernel(
    n, lens, hid_hbm, q_hbm, kv_hbm, new_hbm, gain_hbm, ids_hbm, rw_hbm, wo_hbm, wgu_hbm, wd_hbm,
    out_ref,
    hid, q_ref, new_ref, gain_ref, ids_ref, rw_ref, kv, wo, wgu, wd, load_sem,
    asend, arecv, a_ss, a_rs,
    cz, cg, cz_ss, cz_rs, cg_ss, cg_rs,
    yb, yf, crx, qf, qb, p1rx, q2f, q2b, p2rx, zb, zf, zrx, res,
    rs_ss, rs_rs, z_ss, z_rs,
    nz, gx, nz_ss, nz_rs, ag_ss, ag_rs,
    gu, act, coef,
):
    me = lax.axis_index("dev")
    zc = n // PLANE
    zr = zc * 4
    tokens = 4 * n
    half = tokens // 2
    my_z = lax.div(me, PLANE)
    my_p = lax.rem(me, PLANE)
    my_y = lax.div(my_p, 4)
    my_x = lax.rem(lax.div(my_p, 2), 2)
    my_core = lax.rem(my_p, 2)
    first = (1 - my_core) * my_x + my_core * my_y
    second = (1 - my_core) * my_y + my_core * my_x
    step_x = (1 - 2 * my_x) * 2
    step_y = (1 - 2 * my_y) * 4
    peer1 = me + (1 - my_core) * step_x + my_core * step_y
    peer2 = me + (1 - my_core) * step_y + my_core * step_x
    mate = me + 1 - 2 * my_core
    d_model = out_ref.shape[1]
    cw = d_model // CHUNKS
    sw = cw // SUB
    ctx = kv.shape[1]
    kvw = KVH * HD
    per_group = HEADS // KVH
    hpd = HEADS // n
    dpg = n // KVH
    block = asend.shape[1]

    def z_at(j):
        return lax.rem(my_z + j, zc)

    def z_peer(j):
        return z_at(j) * PLANE + my_p

    barrier = pltpu.get_barrier_semaphore()

    @pl.loop(1, n)
    def _(k):
        pl.semaphore_signal(
            barrier, inc=1, device_id={"dev": lax.rem(me + k, n)},
            device_id_type=pl.DeviceIdType.MESH,
        )

    small = [
        pltpu.make_async_copy(src, dst, load_sem.at[i])
        for i, (src, dst) in enumerate(
            [
                (q_hbm, q_ref), (new_hbm, new_ref), (ids_hbm, ids_ref), (rw_hbm, rw_ref),
                (kv_hbm, kv), (hid_hbm, hid), (gain_hbm, gain_ref),
            ]
        )
    ]
    loads = [
        pltpu.make_async_copy(wo_hbm, wo, load_sem.at[7]),
        pltpu.make_async_copy(wgu_hbm.at[0], wgu, load_sem.at[8]),
        pltpu.make_async_copy(wd_hbm.at[0], wd, load_sem.at[9]),
    ]
    for load in small + loads:
        load.start()
    for load in small[:4]:
        load.wait()

    lane = lax.broadcasted_iota(jnp.int32, (4, 128), 1)
    ids = ids_ref[...]
    rw = rw_ref[...]
    own_coef = jnp.zeros((4, 128), F32)
    for k in range(TOPK):
        own_coef = own_coef + jnp.where(ids[:, k:k + 1] == (lane & 63), rw[:, k:k + 1], 0.0)
    high = own_coef.astype(BF16).astype(F32)
    packed = jnp.where(lane < 64, high, own_coef - high)
    cz[my_z] = jnp.concatenate([packed] * 4, axis=0).astype(BF16)

    rows = per_group * 4
    row_b = lax.broadcasted_iota(jnp.int32, (rows, 1), 0) & 3
    length = jnp.full((rows, 1), lens[0], jnp.int32)
    for b in range(1, 4):
        length = jnp.where(row_b == b, lens[b], length)
    live = lax.broadcasted_iota(jnp.int32, (rows, ctx), 1) < length
    new = new_ref[...].astype(F32)
    for load in small[4:]:
        load.wait()
    for g in range(KVH):
        q_all = q_ref[:, g * per_group * HD:(g + 1) * per_group * HD].astype(F32)
        qg = jnp.concatenate([q_all[:, r * HD:(r + 1) * HD] for r in range(per_group)], axis=0)
        k_own = jnp.concatenate([new[:, g * HD:(g + 1) * HD]] * per_group, axis=0)
        v_own = jnp.concatenate([new[:, kvw + g * HD:kvw + (g + 1) * HD]] * per_group, axis=0)
        q16 = qg.astype(BF16)
        scores = None
        for b in range(4):
            s_b = lax.dot_general(
                q16, kv[b, :, g * HD:(g + 1) * HD], (((1,), (1,)), ((), ())),
                preferred_element_type=F32,
            )
            scores = s_b if b == 0 else jnp.where(row_b == b, s_b, scores)
        scale = HD ** (-0.5)
        scores = jnp.where(live, scores * scale, -jnp.inf)
        fresh = jnp.sum(qg * k_own, axis=1, keepdims=True) * scale
        peak = jnp.maximum(jnp.max(scores, axis=1, keepdims=True), fresh)
        e = jnp.exp(scores - peak)
        e_own = jnp.exp(fresh - peak)
        den = jnp.sum(e, axis=1, keepdims=True) + e_own
        probs = e / den
        p_own = (e_own / den).astype(BF16).astype(F32)
        acc = p_own * v_own
        for b in range(4):
            p_b = jnp.where(row_b == b, probs, 0.0).astype(BF16)
            acc = acc + jnp.dot(
                p_b, kv[b, :, kvw + g * HD:kvw + (g + 1) * HD], preferred_element_type=F32
            )
        for i in range(dpg):
            piece = acc[i * hpd * 4:(i + 1) * hpd * 4, :]
            if piece.shape[0] < block:
                piece = jnp.concatenate([piece] * (block // piece.shape[0]), axis=0)
            asend[g * dpg + i] = piece.astype(BF16)

    pl.semaphore_wait(barrier, n - 1)

    @pl.loop(1, n)
    def _(k):
        target = lax.rem(me + k, n)
        dev_copy(asend.at[target], arecv.at[me], a_ss.at[target], a_rs.at[me], target).start()

    coef_out = []
    for j in range(1, zc):
        copy = dev_copy(
            cz.at[my_z], cz.at[my_z], cz_ss.at[j - 1], cz_rs.at[j - 1], z_peer(j)
        )
        copy.start()
        coef_out.append(copy)

    arecv[me] = asend[me]

    @pl.loop(1, n)
    def _(k):
        source = lax.rem(me + k, n)
        dev_copy(
            asend.at[source], arecv.at[source], a_ss.at[source], a_rs.at[source], source
        ).wait()

    x_all = arecv[...].astype(F32).reshape(n * block, HD).astype(BF16)
    gathered = jnp.concatenate(
        [
            jnp.dot(
                pick_matrix(tokens, n * block, block, rr * 4, zc), x_all,
                preferred_element_type=F32,
            )
            for rr in range(hpd)
        ],
        axis=1,
    ).astype(BF16)

    def reduce_chunks(t, make, done):
        ks = range(CHUNKS)
        cores = [
            dev_copy(
                yb.at[t, k, 1 - my_core], crx.at[t, k], rs_ss.at[t, k, 0], rs_rs.at[t, k, 0], mate
            )
            for k in ks
        ]
        firsts = [
            dev_copy(
                qb.at[t, k, 1 - first], p1rx.at[t, k], rs_ss.at[t, k, 1], rs_rs.at[t, k, 1], peer1
            )
            for k in ks
        ]
        seconds = [
            dev_copy(
                q2b.at[t, k, 1 - second], p2rx.at[t, k], rs_ss.at[t, k, 2], rs_rs.at[t, k, 2], peer2
            )
            for k in ks
        ]
        lines = [
            [
                dev_copy(
                    zb.at[t, k, z_at(j)], zrx.at[t, k, j - 1],
                    z_ss.at[t, k, j - 1], z_rs.at[t, k, j - 1], z_peer(j),
                )
                for j in range(1, zc)
            ]
            for k in range(CHUNKS)
        ]
        for k in range(CHUNKS):
            y = make(k).reshape(2, 2, 2, zr, cw)
            yb[t, k] = y.astype(BF16)
            cores[k].start()
            yf[k] = y
        for k in range(CHUNKS):
            cores[k].wait_recv()
            total = yf[k, my_core] + crx[t, k].astype(F32)
            qb[t, k] = total.astype(BF16)
            firsts[k].start()
            qf[k] = total
        for k in range(CHUNKS):
            firsts[k].wait_recv()
            total = qf[k, first] + p1rx[t, k].astype(F32)
            q2b[t, k] = total.astype(BF16)
            seconds[k].start()
            q2f[k] = total
        for k in range(CHUNKS):
            seconds[k].wait_recv()
            total = q2f[k, second] + p2rx[t, k].astype(F32)
            for z in range(zc):
                part = jnp.concatenate(
                    [total[4 * z:4 * z + 4, s * sw:(s + 1) * sw] for s in range(SUB)], axis=0
                )
                zb[t, k, z] = part.astype(BF16)
                zf[k, z] = part
            for copy in lines[k]:
                copy.start()
        for k in range(CHUNKS):
            total = zf[k, my_z]
            for j in range(1, zc):
                lines[k][j - 1].wait_recv()
                total = total + zrx[t, k, j - 1].astype(F32)
            done(k, total)
        for k in range(CHUNKS):
            for copy in [cores[k], firsts[k], seconds[k]] + lines[k]:
                copy.wait_send()

    for j in range(1, zc):
        from_z = z_at(zc - j)
        dev_copy(
            cz.at[from_z], cz.at[from_z], cz_ss.at[j - 1], cz_rs.at[j - 1], z_peer(j)
        ).wait_recv()
    cg[my_core, first, second] = jnp.concatenate(
        [cz[z].astype(F32)[0:4, :] for z in range(zc)], axis=0
    ).astype(BF16)

    def spread(ref, stage, send, recv):
        here, there, target = [
            (ref.at[my_core, first, second], ref.at[my_core, first, 1 - second], peer2),
            (ref.at[my_core, first], ref.at[my_core, 1 - first], peer1),
            (ref.at[my_core], ref.at[1 - my_core], mate),
        ][stage]
        out = dev_copy(here, here, send, recv, target)
        arrive = dev_copy(there, there, send, recv, target)
        return out, arrive

    coef_steps = [spread(cg, i, cg_ss.at[i], cg_rs.at[i]) for i in range(3)]
    coef_steps[0][0].start()

    loads[0].wait()

    def project(k):
        return jnp.dot(gathered, wo[:, k * cw:(k + 1) * cw], preferred_element_type=F32)

    hidden = hid[...].astype(F32)
    squares = []

    def add_hidden(k, total):
        own = jnp.concatenate(
            [hidden[:, k * cw + s * sw:k * cw + (s + 1) * sw] for s in range(SUB)], axis=0
        )
        value = total + own
        res[k] = value
        squares.append(jnp.sum(value * value, axis=1, keepdims=True))

    reduce_chunks(0, project, add_hidden)

    coef_steps[0][1].wait_recv()
    coef_steps[1][0].start()
    square = sum(squares[1:], squares[0])
    square = square[0:4] + square[4:8] + square[8:12] + square[12:16]
    inverse = lax.rsqrt(square / d_model + 1e-06)
    inverse = jnp.concatenate([inverse] * SUB, axis=0)

    line_out = []
    for k in range(CHUNKS):
        gain = jnp.concatenate(
            [
                jnp.broadcast_to(
                    gain_ref[:, k * cw + s * sw:k * cw + (s + 1) * sw], (4, sw)
                )
                for s in range(SUB)
            ],
            axis=0,
        )
        nz[k, my_z] = (res[k] * inverse * gain).astype(BF16)
        for j in range(1, zc):
            copy = dev_copy(
                nz.at[k, my_z], nz.at[k, my_z], nz_ss.at[k, j - 1], nz_rs.at[k, j - 1], z_peer(j)
            )
            copy.start()
            line_out.append(copy)
    diagonal = peer1 + peer2 - me

    def plane_copies(k):
        here = gx.at[k, my_core, first, second]
        copies = []
        for i, (f, h, target) in enumerate(
            [
                (1 - first, 1 - second, diagonal), (1 - first, second, peer1),
                (first, 1 - second, peer2),
            ]
        ):
            there = gx.at[k, my_core, f, h]
            copies.append(
                (
                    dev_copy(here, here, ag_ss.at[k, i], ag_rs.at[k, i], target),
                    dev_copy(there, there, ag_ss.at[k, i], ag_rs.at[k, i], target),
                )
            )
        return copies

    planes = [plane_copies(k) for k in range(CHUNKS)]
    mates = [spread(gx.at[k], 2, ag_ss.at[k, 3], ag_rs.at[k, 3]) for k in range(CHUNKS)]

    def gather_plane(k):
        for j in range(1, zc):
            from_z = z_at(zc - j)
            dev_copy(
                nz.at[k, from_z], nz.at[k, from_z], nz_ss.at[k, j - 1], nz_rs.at[k, j - 1], z_peer(j)
            ).wait_recv()
        parts = []
        for z in range(zc):
            value = nz[k, z].astype(F32)
            parts.append(
                jnp.concatenate([value[4 * s:4 * s + 4, :] for s in range(SUB)], axis=1)
            )
        gx[k, my_core, first, second] = jnp.concatenate(parts, axis=0).astype(BF16)
        for out, _ in planes[k]:
            out.start()

    def gather_mate(k):
        for _, arrive in planes[k]:
            arrive.wait_recv()
        mates[k][0].start()

    def gate_up(k):
        mates[k][1].wait_recv()
        part = jnp.dot(
            gx[k].reshape(tokens, cw), wgu[k * cw:(k + 1) * cw, :], preferred_element_type=F32
        )
        if k == 0:
            gu[...] = part
        else:
            gu[...] += part

    gathers = [gather_plane, gather_mate, gate_up]
    for at, stage in enumerate(gathers):
        if at == 2:
            loads[1].wait()
            coef_steps[1][1].wait_recv()
            coef_steps[2][0].start()
        for k in range(CHUNKS):
            stage(k)

    coef_steps[2][1].wait_recv()
    lane_t = lax.broadcasted_iota(jnp.int32, (tokens, 128), 1) & 63
    all_coef = cg[...].reshape(tokens, 128).astype(F32)
    coef[...] = jnp.broadcast_to(
        jnp.sum(
            jnp.where(lane_t == lax.div(me, 2), all_coef, 0.0), axis=1, keepdims=True
        ),
        (tokens, 128),
    )

    for copy in line_out + coef_out:
        copy.wait_send()
    for group in planes + [mates, coef_steps]:
        for out, _ in group:
            out.wait_send()
    ff = gu.shape[1] // 2
    gate = gu[:, :ff]
    act[...] = (gate / (1.0 + jnp.exp(-gate)) * gu[:, ff:]).astype(BF16)

    loads[2].wait()

    def expert_out(k):
        y = jnp.dot(act[...], wd[:, k * cw:(k + 1) * cw], preferred_element_type=F32)
        return y.astype(BF16).astype(F32) * coef[:, 0:1]

    def finish(k, total):
        value = (res[k] + total).astype(out_ref.dtype).astype(F32)
        for s in range(SUB):
            lo = k * cw + s * sw
            out_ref[:, lo:lo + sw] = value[4 * s:4 * s + 4, :].astype(out_ref.dtype)

    reduce_chunks(1, expert_out, finish)


def solution(mesh):
    n = mesh.shape["dev"]

    def step(hidden, queries, kv_cache, new_kv, lens, wo, gain, ids, rw, wgu, wd):
        seqs, d_model = hidden.shape
        zc = n // PLANE
        zr = zc * 4
        tokens = n * seqs
        cw = d_model // CHUNKS
        sw = cw // SUB
        block = max(8, HEADS // n * 4)
        dma = pltpu.SemaphoreType.DMA
        vmem = pltpu.VMEM
        any_spec = pl.BlockSpec(memory_space=pl.ANY)
        v_spec = pl.BlockSpec(memory_space=pltpu.VMEM)
        zp = max(1, zc - 1)
        return pl.pallas_call(
            functools.partial(kernel, n),
            out_shape=jax.ShapeDtypeStruct((seqs, d_model), BF16),
            in_specs=[pl.BlockSpec(memory_space=pltpu.SMEM)] + [any_spec] * 10,
            out_specs=v_spec,
            scratch_shapes=[
                vmem(hidden.shape, BF16), vmem(queries.shape, BF16), vmem(new_kv.shape, BF16),
                vmem((1, d_model), F32), vmem(ids.shape, jnp.int32), vmem(rw.shape, F32),
                vmem(kv_cache.shape, BF16), vmem(wo.shape, BF16), vmem(wgu.shape[1:], BF16),
                vmem(wd.shape[1:], BF16), dma((10,)),
                vmem((n, block, HD), BF16), vmem((n, block, HD), BF16), dma((n,)), dma((n,)),
                vmem((zc, 16, 128), BF16), vmem((2, 2, 2, zr, 128), BF16),
                dma((zp,)), dma((zp,)), dma((3,)), dma((3,)),
                vmem((2, CHUNKS, 2, 2, 2, zr, cw), BF16), vmem((CHUNKS, 2, 2, 2, zr, cw), F32),
                vmem((2, CHUNKS, 2, 2, zr, cw), BF16), vmem((CHUNKS, 2, 2, zr, cw), F32),
                vmem((2, CHUNKS, 2, 2, zr, cw), BF16), vmem((2, CHUNKS, 2, zr, cw), BF16),
                vmem((CHUNKS, 2, zr, cw), F32), vmem((2, CHUNKS, 2, zr, cw), BF16),
                vmem((2, CHUNKS, zr, cw), BF16),
                vmem((2, CHUNKS, zc, 4 * SUB, sw), BF16), vmem((CHUNKS, zc, 4 * SUB, sw), F32),
                vmem((2, CHUNKS, zp, 4 * SUB, sw), BF16), vmem((CHUNKS, 4 * SUB, sw), F32),
                dma((2, CHUNKS, 3)), dma((2, CHUNKS, 3)), dma((2, CHUNKS, zp)), dma((2, CHUNKS, zp)),
                vmem((CHUNKS, zc, 4 * SUB, sw), BF16), vmem((CHUNKS, 2, 2, 2, zr, cw), BF16),
                dma((CHUNKS, zp)), dma((CHUNKS, zp)), dma((CHUNKS, 4)), dma((CHUNKS, 4)),
                vmem((tokens, wgu.shape[2]), F32), vmem((tokens, wgu.shape[2] // 2), BF16),
                vmem((tokens, 128), F32),
            ],
            compiler_params=pltpu.CompilerParams(
                collective_id=0, has_side_effects=True, vmem_limit_bytes=60 * 1024 * 1024
            ),
        )(lens, hidden, queries, kv_cache, new_kv, gain.reshape(1, d_model), ids, rw, wo, wgu, wd)

    tok = P(("groups", "dev"), None)
    in_specs = (
        tok, tok, P(("groups", "dev"), None, None), tok, P(("groups", "dev")), P("dev", None),
        P(), tok, tok, P("dev", None, None), P("dev", None, None),
    )
    return jax.shard_map(step, mesh=mesh, in_specs=in_specs, out_specs=tok, check_vma=False)
```
